32 devices in a mesh: parts: 2 (over x), aux: 16 (over z, y, core).
Axes of the slice: x: 2, y: 2, z: 4, core: 2. Of those that a mesh axis runs over, the one named last changes fastest.
Arguments:
- tiles: bfloat16 [32, 8, 8, 128, 128], P(('parts', 'aux')), parts along dimension 0, may hold values from -6 to 6
- mu_list: int32 [32, 8], P(('parts', 'aux')), parts along dimension 0, may hold values from 0 to 7
- lam_list: int32 [32, 8], P(('parts', 'aux')), parts along dimension 0, may hold values from 0 to 7
- tile_count: int32 [32], P(('parts', 'aux')), parts along dimension 0, may hold values from 1 to 8, as said below
- coeff: bfloat16 [2048, 256], P(('parts', 'aux')), parts along dimension 0, may hold values from -0.5 to 0.5
- owner: int32 [32], P('parts'), parts along dimension 0, may hold values from 0 to 15, each once
Outputs:
- exchange: float32 [2048, 1024], P(('parts', 'aux')), parts along dimension 0
The draws below stay inside these ranges and needn't reach their ends.
There are 2 independent parts, one for each index of `parts`. The reference program is written for one: setup_inputs(seed, part) draws one part's arguments, and reference() takes and returns one part's arrays. A program takes and returns all parts, laid end to end along the dimension named above; each array names one. Nothing has to cross between parts.
Inputs may be any that keep to these rules, and one draw needn't show every extreme that they name: Slots from tile_count on are padding and are ignored; in every draw some shard uses all 8 slots.
All inputs are finite; a program needn't handle non-finite values.
Results may differ from the reference program's by a relative error of at most 0.00088.
Values may be sent and summed in bfloat16 or wider, within the bound.
A program may use at most 64 MiB of HBM per device.

```python
import jax
import jax.numpy as jnp
from jax import lax

BS = 128
NB = 8
OCC = 256
PAIRS = 8
AUX_DEV = 8
NBF = 1024
N_AUX = 16


def draw_tile_count(key, part):
    first, second = jax.random.split(jax.random.fold_in(key, 17))
    base = jax.random.randint(first, (N_AUX,), 1, PAIRS // 2 + 1)
    fullest = jax.random.randint(second, (), 0, N_AUX)
    return jnp.where(jnp.arange(N_AUX) == fullest, PAIRS, base).astype(jnp.int32)


def with_ends(values, stream_key, low, high):
    dims = values.shape
    index_at = [jax.random.randint(jax.random.fold_in(stream_key, axis), (), 0, dims[axis]) for axis in range(len(dims))]
    values = values.at[tuple(index_at)].set(low)
    longest = dims.index(max(dims))
    index_at[longest] = (index_at[longest] + 1) % dims[longest]
    return values.at[tuple(index_at)].set(high)


def steps_of(own_key, dims, pieces, low, largest):
    factor_of, own = 1.0, jax.random.fold_in(own_key, 6)
    for dim, parts in pieces:
        steps = jnp.exp(jax.random.uniform(jax.random.fold_in(own, dim), (parts,), jnp.float32, low / len(pieces), largest / len(pieces)))
        factor_of = factor_of * jnp.repeat(steps, dims[dim] // parts).reshape([-1 if axis == dim else 1 for axis in range(len(dims))])
    return factor_of


def centred(rng, extent, deviation, most, cuts=(), held_as=jnp.bfloat16):
    entries = deviation * jax.random.normal(rng, extent, jnp.float32)
    if cuts:
        entries = entries * steps_of(rng, extent, cuts, -0.22, 0.18)
    return jnp.clip(entries, -most, most).astype(held_as)


def setup_inputs(seed: int = 0, part: int = 0) -> dict:
    streams_of = jax.random.split(jax.random.key(seed), 7)
    part_keys = jax.random.split(jax.random.fold_in(streams_of[6], part), 7)
    tiles = centred(part_keys[0], (N_AUX, PAIRS, AUX_DEV, BS, BS), 1.0, 6.0, ((0, 16),))
    mu_list = with_ends(jax.random.randint(part_keys[1], (N_AUX, PAIRS), 0, NB), jax.random.fold_in(part_keys[1], 1), 0, NB - 1).astype(jnp.int32)
    lam_list = with_ends(jax.random.randint(part_keys[2], (N_AUX, PAIRS), 0, NB), jax.random.fold_in(part_keys[2], 1), 0, NB - 1).astype(jnp.int32)
    tile_count = draw_tile_count(jax.random.fold_in(jax.random.fold_in(streams_of[6], part), 71), part)
    coeff = centred(part_keys[4], (NBF, OCC), BS ** -0.5, 0.5, ((0, 16),))
    owner = jax.random.permutation(part_keys[5], N_AUX).astype(jnp.int32)
    return {"tiles": tiles, "mu_list": mu_list, "lam_list": lam_list, "tile_count": tile_count, "coeff": coeff, "owner": owner}


def reference(tiles, mu_list, lam_list, tile_count, coeff, owner):
    tile_rows = NBF // N_AUX
    blocks_c = coeff.reshape(NB, BS, OCC).astype(jnp.float32)
    order = (owner[:, None] * tile_rows + jnp.arange(tile_rows, dtype=jnp.int32)[None, :]).reshape(-1).astype(jnp.int32)

    def shard(total, inputs):
        slab, mus, lams, count = inputs
        half = jnp.zeros((AUX_DEV, NB, BS, OCC), jnp.float32)
        for slot in range(PAIRS):
            piece = jnp.einsum("pml,lo->pmo", slab[slot].astype(jnp.float32), blocks_c[lams[slot]], precision=lax.Precision.HIGHEST)
            weight = (slot < count).astype(jnp.float32)
            current = lax.dynamic_index_in_dim(half, mus[slot], 1, keepdims=False)
            half = lax.dynamic_update_index_in_dim(half, current + weight * piece, mus[slot], 1)
        rounded = half.astype(jnp.bfloat16).reshape(AUX_DEV, NBF, OCC)[:, order, :].astype(jnp.float32)
        total = total + jnp.einsum("prk,psk->rs", rounded, rounded, precision=lax.Precision.HIGHEST)
        return total, None

    total, _ = lax.scan(shard, jnp.zeros((NBF, NBF), jnp.float32), (tiles, mu_list, lam_list, tile_count))
    return total / (AUX_DEV * N_AUX * OCC)
```

```python
import functools

import jax
import jax.numpy as jnp
from jax import lax
from jax.experimental import pallas as pl
from jax.experimental.pallas import tpu as pltpu
from jax.sharding import PartitionSpec as P


def partial_kernel(
    shards, scale, mu_ref, lam_ref, count_ref, owner_ref, tiles_ref, coeff_ref, out_ref, half, total, place
):
    slots, aux_local, block, _ = tiles_ref.shape
    nbasis, occupied = coeff_ref.shape
    nblocks = nbasis // block
    tile_rows = nbasis // shards
    count = count_ref[0]

    @pl.loop(0, shards)
    def _(d):
        place[owner_ref[d]] = d

    @pl.loop(0, nblocks)
    def _(b):
        def add(t, seen):
            hit = (mu_ref[t] == b) & (t < count)

            def term():
                start = pl.multiple_of(lam_ref[t] * block, block)
                return jnp.dot(
                    tiles_ref[t].reshape(aux_local * block, block),
                    coeff_ref[pl.ds(start, block), :],
                    preferred_element_type=jnp.float32,
                )

            @pl.when(hit & (seen == 0))
            def _():
                total[...] = term()

            @pl.when(hit & (seen > 0))
            def _():
                total[...] += term()

            return seen + hit.astype(jnp.int32)

        seen = lax.fori_loop(0, slots, add, jnp.int32(0))
        pieces = max(block // tile_rows, 1)
        rows = block // pieces
        per_tile = tile_rows // rows
        for piece in range(pieces):
            at = b * pieces + piece
            where = pl.multiple_of(place[at // per_tile] * tile_rows + lax.rem(at, per_tile) * rows, rows)

            @pl.when(seen > 0)
            def _():
                for p in range(aux_local):
                    half[pl.ds(where, rows), p * occupied : (p + 1) * occupied] = total[
                        p * block + piece * rows : p * block + (piece + 1) * rows, :
                    ].astype(half.dtype)

            @pl.when(seen == 0)
            def _():
                half[pl.ds(where, rows), :] = jnp.zeros((rows, aux_local * occupied), half.dtype)

    chunk = 256 if nbasis % 256 == 0 else block

    @pl.loop(0, nbasis // chunk)
    def _(r):
        start = pl.multiple_of(r * chunk, chunk)
        out_ref[pl.ds(start, chunk), :] = (
            lax.dot_general(
                half[pl.ds(start, chunk), :],
                half[...],
                (((1,), (1,)), ((), ())),
                preferred_element_type=jnp.float32,
            )
            * scale
        )


def body(tiles, mu_list, lam_list, tile_count, coeff, owner):
    shards = lax.axis_size("aux")
    whole_coeff = lax.all_gather(coeff, "aux", axis=0, tiled=True)
    nbasis, occupied = whole_coeff.shape
    _, slots, aux_local, block, _ = tiles.shape
    smem = pl.BlockSpec(memory_space=pltpu.SMEM)
    vmem = pl.BlockSpec(memory_space=pltpu.VMEM)
    partial = pl.pallas_call(
        functools.partial(partial_kernel, shards, 1.0 / (aux_local * shards * occupied)),
        out_shape=jax.ShapeDtypeStruct((nbasis, nbasis), jnp.float32),
        in_specs=[smem] * 4 + [vmem] * 2,
        out_specs=vmem,
        scratch_shapes=[
            pltpu.VMEM((nbasis, aux_local * occupied), jnp.bfloat16),
            pltpu.VMEM((aux_local * block, occupied), jnp.float32),
            pltpu.SMEM((shards,), jnp.int32),
        ],
        compiler_params=pltpu.CompilerParams(vmem_limit_bytes=48 * 1024 * 1024),
    )(mu_list[0], lam_list[0], tile_count, owner, tiles[0], whole_coeff)
    return lax.psum_scatter(partial, "aux", scatter_dimension=0, tiled=True)


def solution(mesh):
    return jax.shard_map(
        body,
        mesh=mesh,
        in_specs=(
            P(("parts", "aux"), None, None, None, None),
            P(("parts", "aux"), None),
            P(("parts", "aux"), None),
            P(("parts", "aux")),
            P(("parts", "aux"), None),
            P("parts"),
        ),
        out_specs=P(("parts", "aux"), None),
        check_vma=False,
    )
```

```python
import functools

import jax
import jax.numpy as jnp
from jax import lax
from jax.experimental import pallas as pl
from jax.experimental.pallas import tpu as pltpu
from jax.sharding import PartitionSpec as P

MESH = pl.DeviceIdType.MESH


def partial_kernel(
    shards, scale, band, mu_ref, lam_ref, count_ref, owner_ref, tiles_ref, coeff_ref, out_ref, half, total, place
):
    slots, aux_local, block, _ = tiles_ref.shape
    nbasis, occupied = coeff_ref.shape
    nblocks = nbasis // block
    tile_rows = nbasis // shards
    count = count_ref[0]

    @pl.loop(0, shards)
    def _(d):
        place[owner_ref[d]] = d

    @pl.loop(0, nblocks)
    def _(b):
        def add(t, seen):
            hit = (mu_ref[t] == b) & (t < count)

            def term():
                start = pl.multiple_of(lam_ref[t] * block, block)
                return jnp.dot(
                    tiles_ref[t].reshape(aux_local * block, block),
                    coeff_ref[pl.ds(start, block), :],
                    preferred_element_type=jnp.float32,
                )

            @pl.when(hit & (seen == 0))
            def _():
                total[...] = term()

            @pl.when(hit & (seen > 0))
            def _():
                total[...] += term()

            return seen + hit.astype(jnp.int32)

        seen = lax.fori_loop(0, slots, add, jnp.int32(0))
        pieces = max(block // tile_rows, 1)
        rows = block // pieces
        per_tile = tile_rows // rows
        for piece in range(pieces):
            at = b * pieces + piece
            where = pl.multiple_of(place[at // per_tile] * tile_rows + lax.rem(at, per_tile) * rows, rows)

            @pl.when(seen > 0)
            def _():
                for p in range(aux_local):
                    half[pl.ds(where, rows), p * occupied : (p + 1) * occupied] = total[
                        p * block + piece * rows : p * block + (piece + 1) * rows, :
                    ].astype(jnp.bfloat16).astype(half.dtype)

            @pl.when(seen == 0)
            def _():
                half[pl.ds(where, rows), :] = jnp.zeros((rows, aux_local * occupied), half.dtype)

    if band:
        half[nbasis:, :] = half[: half.shape[0] - nbasis, :]

        @pl.loop(0, nblocks)
        def _(d):
            start = pl.multiple_of(d * block, block)
            out_ref[d] = (
                lax.dot_general(
                    half[pl.ds(start, block), :],
                    half[pl.ds(start, band), :],
                    (((1,), (1,)), ((), ())),
                    preferred_element_type=jnp.float32,
                )
                * scale
            )

    else:

        @pl.loop(0, nblocks)
        def _(d):
            start = pl.multiple_of(d * block, block)
            out_ref[pl.ds(start, block), :] = (
                lax.dot_general(
                    half[pl.ds(start, block), :].astype(jnp.bfloat16),
                    half[...].astype(jnp.bfloat16),
                    (((1,), (1,)), ((), ())),
                    preferred_element_type=jnp.float32,
                )
                * scale
            )


def greet(me, shards):
    barrier = pltpu.get_barrier_semaphore()
    for k in range(1, shards):
        pl.semaphore_signal(barrier, inc=1, device_id={"aux": lax.rem(me + k, shards)}, device_id_type=MESH)
    pl.semaphore_wait(barrier, shards - 1)


def push(src, dst, send, recv, device):
    copy = pltpu.make_async_remote_copy(
        src_ref=src, dst_ref=dst, send_sem=send, recv_sem=recv, device_id={"aux": device}, device_id_type=MESH
    )
    copy.start()
    return copy


def gather_kernel(shards, coeff_ref, out_ref, send, recv, pass_send, pass_recv):
    me = lax.axis_index("aux")
    rows = coeff_ref.shape[0]
    chips = shards // 2
    chip, core = me // 2, lax.rem(me, 2)
    sibling = chip * 2 + 1 - core

    def rows_of(device):
        return out_ref.at[pl.ds(pl.multiple_of(device * rows, rows), rows), :]

    greet(me, shards)
    copies = []
    for k in range(1, chips):
        target = lax.rem(chip + k, chips) * 2 + core
        copies.append(push(coeff_ref, rows_of(me), send.at[k], recv.at[k], target))
    passed = [push(coeff_ref, rows_of(me), pass_send.at[0], pass_recv.at[0], sibling)]
    out_ref[pl.ds(pl.multiple_of(me * rows, rows), rows), :] = coeff_ref[...]
    for k in range(1, chips):
        copies[k - 1].wait_recv()
        source = lax.rem(chip + chips - k, chips) * 2 + core
        passed.append(push(rows_of(source), rows_of(source), pass_send.at[k], pass_recv.at[k], sibling))
    for copy in copies:
        copy.wait_send()
    for copy in passed:
        copy.wait()


def scatter_kernel(
    shards, part_ref, out_ref, from_core, to_y, from_y, held, from_z, turned, from_far, core_s, core_r, y_s, y_r, z_s, z_r, far_s, far_r
):
    me = lax.axis_index("aux")
    chips, block, band = part_ref.shape
    rows = block // 2
    depth = chips // 2
    chip, core = me // 2, lax.rem(me, 2)
    z, y = chip // 2, lax.rem(chip, 2)
    sibling = chip * 2 + 1 - core
    mine = pl.ds(pl.multiple_of(core * rows, rows), rows)
    theirs = pl.ds(pl.multiple_of((1 - core) * rows, rows), rows)
    offsets = list(range(depth // 2, 0, -1)) + list(range(depth // 2 + 1, depth)) + [0]

    greet(me, shards)
    cores = {}
    for k in offsets:
        for v in (1, 0):
            d = lax.rem(z + k, depth) * 2 + (y if v == 0 else 1 - y)
            cores[k, v] = push(
                part_ref.at[d, theirs, :], from_core.at[2 * k + v], core_s.at[2 * k + v], core_r.at[2 * k + v], sibling
            )
    ys = {}
    for k in offsets:
        d = lax.rem(z + k, depth) * 2
        cores[k, 1].wait_recv()
        to_y[k] = part_ref[d + 1 - y, mine, :] + from_core[2 * k + 1]
        ys[k] = push(to_y.at[k], from_y.at[k], y_s.at[k], y_r.at[k], (z * 2 + 1 - y) * 2 + core)
        cores[k, 0].wait_recv()
        held[k] = part_ref[d + y, mine, :] + from_core[2 * k]
    zs = {}
    for k in offsets:
        ys[k].wait_recv()
        held[k] += from_y[k]
        if k:
            zs[k] = push(held.at[k], from_z.at[k], z_s.at[k], z_r.at[k], (lax.rem(z + k, depth) * 2 + y) * 2 + core)
    for k in zs:
        zs[k].wait_recv()
        held[0] += from_z[k]

    fars = []
    near = band // block
    for k in range(1, chips - near + 1):
        turned[k - 1] = held[0, :, k * block : (k + 1) * block].T
        for h in range(2):
            n = 2 * (k - 1) + h
            fars.append(
                push(
                    turned.at[k - 1, h * rows : (h + 1) * rows, :],
                    from_far.at[2 * (k - 1) + core],
                    far_s.at[n],
                    far_r.at[2 * (k - 1) + core],
                    lax.rem(chip + k, chips) * 2 + h,
                )
            )
    for k in range(near):
        at = pl.multiple_of(lax.rem(chip + k, chips) * block, block)
        out_ref[:, pl.ds(at, block)] = held[0, :, k * block : (k + 1) * block]
    for copy in fars:
        copy.wait_send()
    for k in range(1, chips - near + 1):
        for c in range(2):
            n = 2 * (k - 1) + c
            pltpu.make_async_copy(from_far.at[n], from_far.at[n], far_r.at[n]).wait()
        at = pl.multiple_of(lax.rem(chip + chips - k, chips) * block, block)
        out_ref[:, pl.ds(at, block)] = jnp.concatenate([from_far[2 * k - 2], from_far[2 * k - 1]], axis=1)
    for group in (cores, ys, zs):
        for copy in group.values():
            copy.wait_send()


def body(tiles, mu_list, lam_list, tile_count, coeff, owner):
    shards = lax.axis_size("aux")
    own_rows, occupied = coeff.shape
    nbasis = own_rows * shards
    _, slots, aux_local, block, _ = tiles.shape
    nblocks = nbasis // block
    smem = pl.BlockSpec(memory_space=pltpu.SMEM)
    vmem = pl.BlockSpec(memory_space=pltpu.VMEM)
    dma = pltpu.SemaphoreType.DMA
    own = own_rows * 2 == block and nblocks % 4 == 0
    band = (nblocks // 2 + 1) * block if own else 0
    if own:
        whole_coeff = pl.pallas_call(
            functools.partial(gather_kernel, shards),
            out_shape=jax.ShapeDtypeStruct((nbasis, occupied), coeff.dtype),
            in_specs=[vmem],
            out_specs=vmem,
            scratch_shapes=[dma((nblocks,))] * 4,
            compiler_params=pltpu.CompilerParams(collective_id=0, has_side_effects=True),
        )(coeff)
    else:
        whole_coeff = lax.all_gather(coeff, "aux", axis=0, tiled=True)
    wide = jnp.bfloat16 if own_rows % 16 == 0 else jnp.float32
    partial = pl.pallas_call(
        functools.partial(partial_kernel, shards, 1.0 / (aux_local * shards * occupied), band),
        out_shape=jax.ShapeDtypeStruct((nblocks, block, band) if own else (nbasis, nbasis), jnp.float32),
        in_specs=[smem] * 4 + [vmem] * 2,
        out_specs=vmem,
        scratch_shapes=[
            pltpu.VMEM((nbasis + max(band - block, 0), aux_local * occupied), wide),
            pltpu.VMEM((aux_local * block, occupied), jnp.float32),
            pltpu.SMEM((shards,), jnp.int32),
        ],
        compiler_params=pltpu.CompilerParams(vmem_limit_bytes=48 * 1024 * 1024),
    )(mu_list[0], lam_list[0], tile_count, owner, tiles[0], whole_coeff)
    if not own:
        return lax.psum_scatter(partial, "aux", scatter_dimension=0, tiled=True)
    depth = nblocks // 2
    far = nblocks - band // block
    f32 = jnp.float32
    return pl.pallas_call(
        functools.partial(scatter_kernel, shards),
        out_shape=jax.ShapeDtypeStruct((own_rows, nbasis), f32),
        in_specs=[vmem],
        out_specs=vmem,
        scratch_shapes=[
            pltpu.VMEM((nblocks, own_rows, band), f32),
            pltpu.VMEM((depth, own_rows, band), f32),
            pltpu.VMEM((depth, own_rows, band), f32),
            pltpu.VMEM((depth, own_rows, band), f32),
            pltpu.VMEM((depth, own_rows, band), f32),
            pltpu.VMEM((far, block, own_rows), f32),
            pltpu.VMEM((2 * far, own_rows, own_rows), f32),
            dma((nblocks,)),
            dma((nblocks,)),
            dma((depth,)),
            dma((depth,)),
            dma((depth,)),
            dma((depth,)),
            dma((2 * far,)),
            dma((2 * far,)),
        ],
        compiler_params=pltpu.CompilerParams(
            collective_id=1, has_side_effects=True, vmem_limit_bytes=32 * 1024 * 1024
        ),
    )(partial)


def solution(mesh):
    return jax.shard_map(
        body,
        mesh=mesh,
        in_specs=(
            P(("parts", "aux"), None, None, None, None),
            P(("parts", "aux"), None),
            P(("parts", "aux"), None),
            P(("parts", "aux")),
            P(("parts", "aux"), None),
            P("parts"),
        ),
        out_specs=P(("parts", "aux"), None),
        check_vma=False,
    )
```

```python
import functools

import jax
import jax.numpy as jnp
from jax import lax
from jax.experimental import pallas as pl
from jax.experimental.pallas import tpu as pltpu
from jax.sharding import PartitionSpec as P

MESH = pl.DeviceIdType.MESH


def partial_kernel(
    shards, scale, own, mu_in, lam_in, count_in, owner_in, tiles_in, coeff_ref, out_ref, *rest
):
    *spare, total, tiles_ref, mu_ref, lam_ref, count_ref, owner_ref, place, sems = rest
    half = out_ref if own else spare[0]
    moves = [
        pltpu.make_async_copy(src, dst, sems.at[n])
        for n, (src, dst) in enumerate(
            (
                (mu_in, mu_ref),
                (lam_in, lam_ref),
                (count_in, count_ref),
                (owner_in, owner_ref),
                (tiles_in, tiles_ref),
            )
        )
    ]
    for move in moves:
        move.start()
    for move in moves:
        move.wait()
    slots, aux_local, block, _ = tiles_ref.shape
    nbasis, occupied = coeff_ref.shape
    nblocks = nbasis // block
    tile_rows = nbasis // shards
    count = count_ref[0]

    @pl.loop(0, shards)
    def _(d):
        place[owner_ref[d]] = d

    @pl.loop(0, nblocks)
    def _(b):
        def add(t, seen):
            hit = (mu_ref[t] == b) & (t < count)

            def term():
                start = pl.multiple_of(lam_ref[t] * block, block)
                return jnp.dot(
                    tiles_ref[t].reshape(aux_local * block, block),
                    coeff_ref[pl.ds(start, block), :],
                    preferred_element_type=jnp.float32,
                )

            @pl.when(hit & (seen == 0))
            def _():
                total[...] = term()

            @pl.when(hit & (seen > 0))
            def _():
                total[...] += term()

            return seen + hit.astype(jnp.int32)

        seen = lax.fori_loop(0, slots, add, jnp.int32(0))
        pieces = max(block // tile_rows, 1)
        rows = block // pieces
        per_tile = tile_rows // rows
        for piece in range(pieces):
            at = b * pieces + piece
            where = pl.multiple_of(place[at // per_tile] * tile_rows + lax.rem(at, per_tile) * rows, rows)

            @pl.when(seen > 0)
            def _():
                for p in range(aux_local):
                    half[pl.ds(where, rows), p * occupied : (p + 1) * occupied] = total[
                        p * block + piece * rows : p * block + (piece + 1) * rows, :
                    ].astype(jnp.bfloat16).astype(half.dtype)

            @pl.when(seen == 0)
            def _():
                half[pl.ds(where, rows), :] = jnp.zeros((rows, aux_local * occupied), half.dtype)

    if own:
        half[nbasis:, :] = half[: half.shape[0] - nbasis, :]
    else:

        @pl.loop(0, nblocks)
        def _(d):
            start = pl.multiple_of(d * block, block)
            out_ref[pl.ds(start, block), :] = (
                lax.dot_general(
                    half[pl.ds(start, block), :].astype(jnp.bfloat16),
                    half[...].astype(jnp.bfloat16),
                    (((1,), (1,)), ((), ())),
                    preferred_element_type=jnp.float32,
                )
                * scale
            )


def greet(me, shards):
    barrier = pltpu.get_barrier_semaphore()
    for k in range(1, shards):
        pl.semaphore_signal(barrier, inc=1, device_id={"aux": lax.rem(me + k, shards)}, device_id_type=MESH)
    pl.semaphore_wait(barrier, shards - 1)


def push(src, dst, send, recv, device):
    copy = pltpu.make_async_remote_copy(
        src_ref=src, dst_ref=dst, send_sem=send, recv_sem=recv, device_id={"aux": device}, device_id_type=MESH
    )
    copy.start()
    return copy


def gather_kernel(shards, coeff_ref, out_ref, send, recv, pass_send, pass_recv):
    me = lax.axis_index("aux")
    rows = coeff_ref.shape[0]
    chips = shards // 2
    chip, core = me // 2, lax.rem(me, 2)
    sibling = chip * 2 + 1 - core

    def rows_of(device):
        return out_ref.at[pl.ds(pl.multiple_of(device * rows, rows), rows), :]

    greet(me, shards)
    copies = []
    for k in range(1, chips):
        target = lax.rem(chip + k, chips) * 2 + core
        copies.append(push(coeff_ref, rows_of(me), send.at[k], recv.at[k], target))
    passed = [push(coeff_ref, rows_of(me), pass_send.at[0], pass_recv.at[0], sibling)]
    out_ref[pl.ds(pl.multiple_of(me * rows, rows), rows), :] = coeff_ref[...]
    for k in range(1, chips):
        copies[k - 1].wait_recv()
        source = lax.rem(chip + chips - k, chips) * 2 + core
        passed.append(push(rows_of(source), rows_of(source), pass_send.at[k], pass_recv.at[k], sibling))
    for copy in copies:
        copy.wait_send()
    for copy in passed:
        copy.wait()


def scatter_kernel(
    shards, scale, half_ref, out_ref, part_ref, from_core, to_y, from_y, held, from_z, turned, from_far, core_s, core_r, y_s, y_r, z_s, z_r, far_s, far_r
):
    me = lax.axis_index("aux")
    chips, block, band = part_ref.shape
    rows = block // 2
    depth = chips // 2
    chip, core = me // 2, lax.rem(me, 2)
    z, y = chip // 2, lax.rem(chip, 2)
    sibling = chip * 2 + 1 - core
    mine = pl.ds(pl.multiple_of(core * rows, rows), rows)
    theirs = pl.ds(pl.multiple_of((1 - core) * rows, rows), rows)
    offsets = list(range(depth // 2, 0, -1)) + list(range(depth // 2 + 1, depth)) + [0]

    greet(me, shards)
    cores, ys = {}, {}

    def multiply(k, v):
        n = 2 * k + v
        d = lax.rem(z + k, depth) * 2 + (y if v == 0 else 1 - y)
        start = pl.multiple_of(d * block, block)
        part_ref[n] = (
            lax.dot_general(
                half_ref[pl.ds(start, block), :],
                half_ref[pl.ds(start, band), :],
                (((1,), (1,)), ((), ())),
                preferred_element_type=jnp.float32,
            )
            * scale
        )
        cores[k, v] = push(part_ref.at[n, theirs, :], from_core.at[n], core_s.at[n], core_r.at[n], sibling)

    def send_on(k):
        cores[k, 1].wait_recv()
        to_y[k] = part_ref[2 * k + 1, mine, :] + from_core[2 * k + 1]
        ys[k] = push(to_y.at[k], from_y.at[k], y_s.at[k], y_r.at[k], (z * 2 + 1 - y) * 2 + core)

    before = None
    for k in offsets:
        multiply(k, 1)
        if before is not None:
            send_on(before)
        before = k
    send_on(before)
    for k in offsets:
        multiply(k, 0)
    zs = {}
    for k in offsets:
        cores[k, 0].wait_recv()
        ys[k].wait_recv()
        held[k] = part_ref[2 * k, mine, :] + from_core[2 * k] + from_y[k]
        if k:
            zs[k] = push(held.at[k], from_z.at[k], z_s.at[k], z_r.at[k], (lax.rem(z + k, depth) * 2 + y) * 2 + core)
    for k in zs:
        zs[k].wait_recv()
        held[0] += from_z[k]

    fars = []
    near = band // block
    for k in range(1, chips - near + 1):
        turned[k - 1] = held[0, :, k * block : (k + 1) * block].T
        for h in range(2):
            n = 2 * (k - 1) + h
            fars.append(
                push(
                    turned.at[k - 1, h * rows : (h + 1) * rows, :],
                    from_far.at[2 * (k - 1) + core],
                    far_s.at[n],
                    far_r.at[2 * (k - 1) + core],
                    lax.rem(chip + k, chips) * 2 + h,
                )
            )
    for k in range(near):
        at = pl.multiple_of(lax.rem(chip + k, chips) * block, block)
        out_ref[:, pl.ds(at, block)] = held[0, :, k * block : (k + 1) * block]
    for copy in fars:
        copy.wait_send()
    for k in range(1, chips - near + 1):
        for c in range(2):
            n = 2 * (k - 1) + c
            pltpu.make_async_copy(from_far.at[n], from_far.at[n], far_r.at[n]).wait()
        at = pl.multiple_of(lax.rem(chip + chips - k, chips) * block, block)
        out_ref[:, pl.ds(at, block)] = jnp.concatenate([from_far[2 * k - 2], from_far[2 * k - 1]], axis=1)
    for group in (cores, ys, zs):
        for copy in group.values():
            copy.wait_send()


def body(tiles, mu_list, lam_list, tile_count, coeff, owner):
    shards = lax.axis_size("aux")
    own_rows, occupied = coeff.shape
    nbasis = own_rows * shards
    _, slots, aux_local, block, _ = tiles.shape
    nblocks = nbasis // block
    depth_of_sum = aux_local * occupied
    scale = 1.0 / (depth_of_sum * shards)
    vmem = pl.BlockSpec(memory_space=pltpu.VMEM)
    dma = pltpu.SemaphoreType.DMA
    own = own_rows * 2 == block and nblocks % 4 == 0
    band = (nblocks // 2 + 1) * block if own else 0
    if own:
        whole_coeff = pl.pallas_call(
            functools.partial(gather_kernel, shards),
            out_shape=pltpu.VMEM((nbasis, occupied), coeff.dtype),
            in_specs=[vmem],
            out_specs=vmem,
            scratch_shapes=[dma((nblocks,))] * 4,
            compiler_params=pltpu.CompilerParams(collective_id=0, has_side_effects=True),
        )(coeff)
    else:
        whole_coeff = lax.all_gather(coeff, "aux", axis=0, tiled=True)
    wide = jnp.bfloat16 if own_rows % 16 == 0 else jnp.float32
    partial = pl.pallas_call(
        functools.partial(partial_kernel, shards, scale, own),
        out_shape=pltpu.VMEM((nbasis + band - block, depth_of_sum), jnp.bfloat16)
        if own
        else jax.ShapeDtypeStruct((nbasis, nbasis), jnp.float32),
        in_specs=[pl.BlockSpec(memory_space=pltpu.HBM)] * 5 + [vmem],
        out_specs=vmem,
        scratch_shapes=([] if own else [pltpu.VMEM((nbasis, depth_of_sum), wide)])
        + [
            pltpu.VMEM((aux_local * block, occupied), jnp.float32),
            pltpu.VMEM((slots, aux_local, block, block), tiles.dtype),
            pltpu.SMEM((slots,), jnp.int32),
            pltpu.SMEM((slots,), jnp.int32),
            pltpu.SMEM((1,), jnp.int32),
            pltpu.SMEM((shards,), jnp.int32),
            pltpu.SMEM((shards,), jnp.int32),
            dma((5,)),
        ],
        compiler_params=pltpu.CompilerParams(vmem_limit_bytes=(56 if own else 48) * 1024 * 1024),
    )(mu_list[0], lam_list[0], tile_count, owner, tiles[0], whole_coeff)
    if not own:
        return lax.psum_scatter(partial, "aux", scatter_dimension=0, tiled=True)
    depth = nblocks // 2
    far = nblocks - band // block
    f32 = jnp.float32
    return pl.pallas_call(
        functools.partial(scatter_kernel, shards, scale),
        out_shape=jax.ShapeDtypeStruct((own_rows, nbasis), f32),
        in_specs=[vmem],
        out_specs=vmem,
        scratch_shapes=[
            pltpu.VMEM((nblocks, block, band), f32),
            pltpu.VMEM((nblocks, own_rows, band), f32),
            pltpu.VMEM((depth, own_rows, band), f32),
            pltpu.VMEM((depth, own_rows, band), f32),
            pltpu.VMEM((depth, own_rows, band), f32),
            pltpu.VMEM((depth, own_rows, band), f32),
            pltpu.VMEM((far, block, own_rows), f32),
            pltpu.VMEM((2 * far, own_rows, own_rows), f32),
            dma((nblocks,)),
            dma((nblocks,)),
            dma((depth,)),
            dma((depth,)),
            dma((depth,)),
            dma((depth,)),
            dma((2 * far,)),
            dma((2 * far,)),
        ],
        compiler_params=pltpu.CompilerParams(
            collective_id=1, has_side_effects=True, vmem_limit_bytes=24 * 1024 * 1024
        ),
    )(partial)


def solution(mesh):
    return jax.shard_map(
        body,
        mesh=mesh,
        in_specs=(
            P(("parts", "aux"), None, None, None, None),
            P(("parts", "aux"), None),
            P(("parts", "aux"), None),
            P(("parts", "aux")),
            P(("parts", "aux"), None),
            P("parts"),
        ),
        out_specs=P(("parts", "aux"), None),
        check_vma=False,
    )
```

```python
import functools

import jax
import jax.numpy as jnp
from jax import lax
from jax.experimental import pallas as pl
from jax.experimental.pallas import tpu as pltpu
from jax.sharding import PartitionSpec as P

MESH = pl.DeviceIdType.MESH


def partial_kernel(
    shards, scale, own, mu_in, lam_in, count_in, owner_in, tiles_in, coeff_ref, out_ref, *rest
):
    *spare, total, tiles_ref, mu_ref, lam_ref, count_ref, owner_ref, place, sems = rest
    half = out_ref if own else spare[0]
    moves = [
        pltpu.make_async_copy(src, dst, sems.at[n])
        for n, (src, dst) in enumerate(
            (
                (mu_in, mu_ref),
                (lam_in, lam_ref),
                (count_in, count_ref),
                (owner_in, owner_ref),
                (tiles_in, tiles_ref),
            )
        )
    ]
    for move in moves:
        move.start()
    for move in moves:
        move.wait()
    slots, aux_local, block, _ = tiles_ref.shape
    nbasis, occupied = coeff_ref.shape
    nblocks = nbasis // block
    tile_rows = nbasis // shards
    count = count_ref[0]

    @pl.loop(0, shards)
    def _(d):
        place[owner_ref[d]] = d

    @pl.loop(0, nblocks)
    def _(b):
        def add(t, seen):
            hit = (mu_ref[t] == b) & (t < count)

            def term():
                start = pl.multiple_of(lam_ref[t] * block, block)
                return jnp.dot(
                    tiles_ref[t].reshape(aux_local * block, block),
                    coeff_ref[pl.ds(start, block), :],
                    preferred_element_type=jnp.float32,
                )

            @pl.when(hit & (seen == 0))
            def _():
                total[...] = term()

            @pl.when(hit & (seen > 0))
            def _():
                total[...] += term()

            return seen + hit.astype(jnp.int32)

        seen = lax.fori_loop(0, slots, add, jnp.int32(0))
        pieces = max(block // tile_rows, 1)
        rows = block // pieces
        per_tile = tile_rows // rows
        for piece in range(pieces):
            at = b * pieces + piece
            where = pl.multiple_of(place[at // per_tile] * tile_rows + lax.rem(at, per_tile) * rows, rows)

            @pl.when(seen > 0)
            def _():
                for p in range(aux_local):
                    half[pl.ds(where, rows), p * occupied : (p + 1) * occupied] = total[
                        p * block + piece * rows : p * block + (piece + 1) * rows, :
                    ].astype(jnp.bfloat16).astype(half.dtype)

            @pl.when(seen == 0)
            def _():
                half[pl.ds(where, rows), :] = jnp.zeros((rows, aux_local * occupied), half.dtype)

    if own:
        half[nbasis:, :] = half[: half.shape[0] - nbasis, :]
    else:

        @pl.loop(0, nblocks)
        def _(d):
            start = pl.multiple_of(d * block, block)
            out_ref[pl.ds(start, block), :] = (
                lax.dot_general(
                    half[pl.ds(start, block), :].astype(jnp.bfloat16),
                    half[...].astype(jnp.bfloat16),
                    (((1,), (1,)), ((), ())),
                    preferred_element_type=jnp.float32,
                )
                * scale
            )


def greet(me, shards):
    barrier = pltpu.get_barrier_semaphore()
    for k in range(1, shards):
        pl.semaphore_signal(barrier, inc=1, device_id={"aux": lax.rem(me + k, shards)}, device_id_type=MESH)
    return lambda: pl.semaphore_wait(barrier, shards - 1)


def push(src, dst, send, recv, device):
    copy = pltpu.make_async_remote_copy(
        src_ref=src, dst_ref=dst, send_sem=send, recv_sem=recv, device_id={"aux": device}, device_id_type=MESH
    )
    copy.start()
    return copy


def gather_kernel(shards, coeff_ref, out_ref, send, recv, pass_send, pass_recv):
    me = lax.axis_index("aux")
    rows = coeff_ref.shape[0]
    chips = shards // 2
    chip, core = me // 2, lax.rem(me, 2)
    sibling = chip * 2 + 1 - core

    def rows_of(device):
        return out_ref.at[pl.ds(pl.multiple_of(device * rows, rows), rows), :]

    met = greet(me, shards)
    out_ref[pl.ds(pl.multiple_of(me * rows, rows), rows), :] = coeff_ref[...]
    met()
    copies = []
    for k in range(1, chips):
        target = lax.rem(chip + k, chips) * 2 + core
        copies.append(push(coeff_ref, rows_of(me), send.at[k], recv.at[k], target))
    passed = [push(coeff_ref, rows_of(me), pass_send.at[0], pass_recv.at[0], sibling)]
    for k in range(1, chips):
        copies[k - 1].wait_recv()
        source = lax.rem(chip + chips - k, chips) * 2 + core
        passed.append(push(rows_of(source), rows_of(source), pass_send.at[k], pass_recv.at[k], sibling))
    for copy in copies:
        copy.wait_send()
    for copy in passed:
        copy.wait()


def scatter_kernel(
    shards, scale, half_ref, out_ref, part_ref, from_core, to_y, from_y, held, from_z, turned, from_far, core_s, core_r, y_s, y_r, z_s, z_r, far_s, far_r
):
    me = lax.axis_index("aux")
    chips, block, band = part_ref.shape
    rows = block // 2
    depth = chips // 2
    chip, core = me // 2, lax.rem(me, 2)
    z, y = chip // 2, lax.rem(chip, 2)
    sibling = chip * 2 + 1 - core
    mine = pl.ds(pl.multiple_of(core * rows, rows), rows)
    theirs = pl.ds(pl.multiple_of((1 - core) * rows, rows), rows)
    offsets = list(range(depth // 2, 0, -1)) + list(range(depth // 2 + 1, depth)) + [0]

    met = greet(me, shards)
    cores, ys = {}, {}

    def multiply(k, v):
        n = 2 * k + v
        d = lax.rem(z + k, depth) * 2 + (y if v == 0 else 1 - y)
        start = pl.multiple_of(d * block, block)
        part_ref[n] = (
            lax.dot_general(
                half_ref[pl.ds(start, block), :],
                half_ref[pl.ds(start, band), :],
                (((1,), (1,)), ((), ())),
                preferred_element_type=jnp.float32,
            )
            * scale
        )
        if (k, v) == (offsets[0], 1):
            met()
        cores[k, v] = push(part_ref.at[n, theirs, :], from_core.at[n], core_s.at[n], core_r.at[n], sibling)

    def send_on(k):
        cores[k, 1].wait_recv()
        to_y[k] = part_ref[2 * k + 1, mine, :] + from_core[2 * k + 1]
        ys[k] = push(to_y.at[k], from_y.at[k], y_s.at[k], y_r.at[k], (z * 2 + 1 - y) * 2 + core)

    before = None
    for k in offsets:
        multiply(k, 1)
        if before is not None:
            send_on(before)
        before = k
    send_on(before)
    for k in offsets:
        multiply(k, 0)
    zs = {}
    for k in offsets:
        cores[k, 0].wait_recv()
        ys[k].wait_recv()
        held[k] = part_ref[2 * k, mine, :] + from_core[2 * k] + from_y[k]
        if k:
            zs[k] = push(held.at[k], from_z.at[k], z_s.at[k], z_r.at[k], (lax.rem(z + k, depth) * 2 + y) * 2 + core)
    for k in zs:
        zs[k].wait_recv()
        held[0] += from_z[k]

    fars = []
    near = band // block
    for k in range(1, chips - near + 1):
        flipped = held[0, :, k * block : (k + 1) * block].T
        for h in range(2):
            low = h * rows
            turned[2 * (k - 1) + h] = jnp.concatenate(
                [flipped[low : low + rows // 2, :], flipped[low + rows // 2 : low + rows, :]], axis=1
            )
            n = 2 * (k - 1) + h
            fars.append(
                push(
                    turned.at[n],
                    from_far.at[2 * (k - 1) + core],
                    far_s.at[n],
                    far_r.at[2 * (k - 1) + core],
                    lax.rem(chip + k, chips) * 2 + h,
                )
            )
    for k in range(near):
        at = pl.multiple_of(lax.rem(chip + k, chips) * block, block)
        out_ref[:, pl.ds(at, block)] = held[0, :, k * block : (k + 1) * block]
    for copy in fars:
        copy.wait_send()
    for k in range(1, chips - near + 1):
        for c in range(2):
            n = 2 * (k - 1) + c
            pltpu.make_async_copy(from_far.at[n], from_far.at[n], far_r.at[n]).wait()
        at = pl.multiple_of(lax.rem(chip + chips - k, chips) * block, block)
        first, second = from_far[2 * k - 2], from_far[2 * k - 1]
        out_ref[: rows // 2, pl.ds(at, block)] = jnp.concatenate([first[:, :rows], second[:, :rows]], axis=1)
        out_ref[rows // 2 :, pl.ds(at, block)] = jnp.concatenate([first[:, rows:], second[:, rows:]], axis=1)
    for group in (cores, ys, zs):
        for copy in group.values():
            copy.wait_send()


def body(tiles, mu_list, lam_list, tile_count, coeff, owner):
    shards = lax.axis_size("aux")
    own_rows, occupied = coeff.shape
    nbasis = own_rows * shards
    _, slots, aux_local, block, _ = tiles.shape
    nblocks = nbasis // block
    depth_of_sum = aux_local * occupied
    scale = 1.0 / (depth_of_sum * shards)
    vmem = pl.BlockSpec(memory_space=pltpu.VMEM)
    dma = pltpu.SemaphoreType.DMA
    own = own_rows * 2 == block and nblocks % 4 == 0
    band = (nblocks // 2 + 1) * block if own else 0
    if own:
        whole_coeff = pl.pallas_call(
            functools.partial(gather_kernel, shards),
            out_shape=pltpu.VMEM((nbasis, occupied), coeff.dtype),
            in_specs=[vmem],
            out_specs=vmem,
            scratch_shapes=[dma((nblocks,))] * 4,
            compiler_params=pltpu.CompilerParams(collective_id=0, has_side_effects=True),
        )(coeff)
    else:
        whole_coeff = lax.all_gather(coeff, "aux", axis=0, tiled=True)
    wide = jnp.bfloat16 if own_rows % 16 == 0 else jnp.float32
    partial = pl.pallas_call(
        functools.partial(partial_kernel, shards, scale, own),
        out_shape=pltpu.VMEM((nbasis + band - block, depth_of_sum), jnp.bfloat16)
        if own
        else jax.ShapeDtypeStruct((nbasis, nbasis), jnp.float32),
        in_specs=[pl.BlockSpec(memory_space=pltpu.HBM)] * 5 + [vmem],
        out_specs=vmem,
        scratch_shapes=([] if own else [pltpu.VMEM((nbasis, depth_of_sum), wide)])
        + [
            pltpu.VMEM((aux_local * block, occupied), jnp.float32),
            pltpu.VMEM((slots, aux_local, block, block), tiles.dtype),
            pltpu.SMEM((slots,), jnp.int32),
            pltpu.SMEM((slots,), jnp.int32),
            pltpu.SMEM((1,), jnp.int32),
            pltpu.SMEM((shards,), jnp.int32),
            pltpu.SMEM((shards,), jnp.int32),
            dma((5,)),
        ],
        compiler_params=pltpu.CompilerParams(vmem_limit_bytes=(56 if own else 48) * 1024 * 1024),
    )(mu_list[0], lam_list[0], tile_count, owner, tiles[0], whole_coeff)
    if not own:
        return lax.psum_scatter(partial, "aux", scatter_dimension=0, tiled=True)
    depth = nblocks // 2
    far = nblocks - band // block
    f32 = jnp.float32
    return pl.pallas_call(
        functools.partial(scatter_kernel, shards, scale),
        out_shape=jax.ShapeDtypeStruct((own_rows, nbasis), f32),
        in_specs=[vmem],
        out_specs=vmem,
        scratch_shapes=[
            pltpu.VMEM((nblocks, block, band), f32),
            pltpu.VMEM((nblocks, own_rows, band), f32),
            pltpu.VMEM((depth, own_rows, band), f32),
            pltpu.VMEM((depth, own_rows, band), f32),
            pltpu.VMEM((depth, own_rows, band), f32),
            pltpu.VMEM((depth, own_rows, band), f32),
            pltpu.VMEM((2 * far, own_rows // 2, block), f32),
            pltpu.VMEM((2 * far, own_rows // 2, block), f32),
            dma((nblocks,)),
            dma((nblocks,)),
            dma((depth,)),
            dma((depth,)),
            dma((depth,)),
            dma((depth,)),
            dma((2 * far,)),
            dma((2 * far,)),
        ],
        compiler_params=pltpu.CompilerParams(
            collective_id=1, has_side_effects=True, vmem_limit_bytes=24 * 1024 * 1024
        ),
    )(partial)


def solution(mesh):
    return jax.shard_map(
        body,
        mesh=mesh,
        in_specs=(
            P(("parts", "aux"), None, None, None, None),
            P(("parts", "aux"), None),
            P(("parts", "aux"), None),
            P(("parts", "aux")),
            P(("parts", "aux"), None),
            P("parts"),
        ),
        out_specs=P(("parts", "aux"), None),
        check_vma=False,
    )
```

```python
import functools

import jax
import jax.numpy as jnp
from jax import lax
from jax.experimental import pallas as pl
from jax.experimental.pallas import tpu as pltpu
from jax.sharding import PartitionSpec as P

MESH = pl.DeviceIdType.MESH


def partial_kernel(
    shards, scale, own, mu_in, lam_in, count_in, owner_in, tiles_in, coeff_ref, out_ref, *rest
):
    *spare, total, tiles_ref, mu_ref, lam_ref, count_ref, owner_ref, place, sems = rest
    half = out_ref if own else spare[0]
    moves = [
        pltpu.make_async_copy(src, dst, sems.at[n])
        for n, (src, dst) in enumerate(
            (
                (mu_in, mu_ref),
                (lam_in, lam_ref),
                (count_in, count_ref),
                (owner_in, owner_ref),
                (tiles_in, tiles_ref),
            )
        )
    ]
    for move in moves:
        move.start()
    for move in moves:
        move.wait()
    slots, aux_local, block, _ = tiles_ref.shape
    nbasis, occupied = coeff_ref.shape
    nblocks = nbasis // block
    tile_rows = nbasis // shards
    count = count_ref[0]

    @pl.loop(0, shards)
    def _(d):
        place[owner_ref[d]] = d

    @pl.loop(0, nblocks)
    def _(b):
        def add(t, seen):
            hit = (mu_ref[t] == b) & (t < count)

            def term():
                start = pl.multiple_of(lam_ref[t] * block, block)
                return jnp.dot(
                    tiles_ref[t].reshape(aux_local * block, block),
                    coeff_ref[pl.ds(start, block), :],
                    preferred_element_type=jnp.float32,
                )

            @pl.when(hit & (seen == 0))
            def _():
                total[...] = term()

            @pl.when(hit & (seen > 0))
            def _():
                total[...] += term()

            return seen + hit.astype(jnp.int32)

        seen = lax.fori_loop(0, slots, add, jnp.int32(0))
        pieces = max(block // tile_rows, 1)
        rows = block // pieces
        per_tile = tile_rows // rows
        for piece in range(pieces):
            at = b * pieces + piece
            where = pl.multiple_of(place[at // per_tile] * tile_rows + lax.rem(at, per_tile) * rows, rows)

            @pl.when(seen > 0)
            def _():
                for p in range(aux_local):
                    half[pl.ds(where, rows), p * occupied : (p + 1) * occupied] = total[
                        p * block + piece * rows : p * block + (piece + 1) * rows, :
                    ].astype(jnp.bfloat16).astype(half.dtype)

            @pl.when(seen == 0)
            def _():
                half[pl.ds(where, rows), :] = jnp.zeros((rows, aux_local * occupied), half.dtype)

    if own:
        half[nbasis:, :] = half[: half.shape[0] - nbasis, :]
    else:

        @pl.loop(0, nblocks)
        def _(d):
            start = pl.multiple_of(d * block, block)
            out_ref[pl.ds(start, block), :] = (
                lax.dot_general(
                    half[pl.ds(start, block), :].astype(jnp.bfloat16),
                    half[...].astype(jnp.bfloat16),
                    (((1,), (1,)), ((), ())),
                    preferred_element_type=jnp.float32,
                )
                * scale
            )


def greet(me, shards):
    barrier = pltpu.get_barrier_semaphore()
    for k in range(1, shards):
        pl.semaphore_signal(barrier, inc=1, device_id={"aux": lax.rem(me + k, shards)}, device_id_type=MESH)
    return lambda: pl.semaphore_wait(barrier, shards - 1)


def push(src, dst, send, recv, device):
    copy = pltpu.make_async_remote_copy(
        src_ref=src, dst_ref=dst, send_sem=send, recv_sem=recv, device_id={"aux": device}, device_id_type=MESH
    )
    copy.start()
    return copy


def gather_kernel(shards, coeff_ref, out_ref, send, recv, pass_send, pass_recv):
    me = lax.axis_index("aux")
    rows = coeff_ref.shape[0]
    chips = shards // 2
    chip, core = me // 2, lax.rem(me, 2)
    sibling = chip * 2 + 1 - core

    def rows_of(device):
        return out_ref.at[pl.ds(pl.multiple_of(device * rows, rows), rows), :]

    met = greet(me, shards)
    out_ref[pl.ds(pl.multiple_of(me * rows, rows), rows), :] = coeff_ref[...]
    met()
    copies = {}
    near_first = sorted(range(1, chips), key=lambda k: min(k, chips - k))
    for k in near_first[::-1]:
        target = lax.rem(chip + k, chips) * 2 + core
        copies[k] = push(coeff_ref, rows_of(me), send.at[k], recv.at[k], target)
    passed = [push(coeff_ref, rows_of(me), pass_send.at[0], pass_recv.at[0], sibling)]
    for k in near_first:
        copies[k].wait_recv()
        source = lax.rem(chip + chips - k, chips) * 2 + core
        passed.append(push(rows_of(source), rows_of(source), pass_send.at[k], pass_recv.at[k], sibling))
    for copy in copies.values():
        copy.wait_send()
    for copy in passed:
        copy.wait()


def scatter_kernel(
    shards, scale, half_ref, out_ref, part_ref, from_core, to_y, from_y, held, from_z, turned, from_far, core_s, core_r, y_s, y_r, z_s, z_r, far_s, far_r
):
    me = lax.axis_index("aux")
    chips, block, band = part_ref.shape
    rows = block // 2
    depth = chips // 2
    chip, core = me // 2, lax.rem(me, 2)
    z, y = chip // 2, lax.rem(chip, 2)
    sibling = chip * 2 + 1 - core
    mine = pl.ds(pl.multiple_of(core * rows, rows), rows)
    theirs = pl.ds(pl.multiple_of((1 - core) * rows, rows), rows)
    offsets = list(range(depth // 2, 0, -1)) + list(range(depth // 2 + 1, depth)) + [0]

    met = greet(me, shards)
    cores, ys = {}, {}

    def multiply(k, v):
        n = 2 * k + v
        d = lax.rem(z + k, depth) * 2 + (y if v == 0 else 1 - y)
        start = pl.multiple_of(d * block, block)
        part_ref[n] = (
            lax.dot_general(
                half_ref[pl.ds(start, block), :],
                half_ref[pl.ds(start, band), :],
                (((1,), (1,)), ((), ())),
                preferred_element_type=jnp.float32,
            )
            * scale
        )
        if (k, v) == (offsets[0], 1):
            met()
        cores[k, v] = push(part_ref.at[n, theirs, :], from_core.at[n], core_s.at[n], core_r.at[n], sibling)

    def send_on(k):
        cores[k, 1].wait_recv()
        to_y[k] = part_ref[2 * k + 1, mine, :] + from_core[2 * k + 1]
        ys[k] = push(to_y.at[k], from_y.at[k], y_s.at[k], y_r.at[k], (z * 2 + 1 - y) * 2 + core)

    before = None
    for k in offsets:
        multiply(k, 1)
        if before is not None:
            send_on(before)
        before = k
    send_on(before)
    for k in offsets:
        multiply(k, 0)
    zs = {}
    near = band // block
    middle = (chips - near + 1) * block
    pieces = ((block, middle), (0, block), (middle, band))
    for k in offsets:
        cores[k, 0].wait_recv()
        ys[k].wait_recv()
        held[k] = part_ref[2 * k, mine, :] + from_core[2 * k] + from_y[k]
        if k:
            for i, (low, high) in enumerate(pieces):
                zs[k, i] = push(
                    held.at[k, :, low:high],
                    from_z.at[k, :, low:high],
                    z_s.at[3 * k + i],
                    z_r.at[3 * k + i],
                    (lax.rem(z + k, depth) * 2 + y) * 2 + core,
                )

    def gather_sums(i):
        low, high = pieces[i]
        for k in offsets[:-1]:
            zs[k, i].wait_recv()
            held[0, :, low:high] += from_z[k, :, low:high]

    gather_sums(0)
    fars = []
    for k in range(1, chips - near + 1):
        flipped = held[0, :, k * block : (k + 1) * block].T
        for h in range(2):
            low = h * rows
            turned[2 * (k - 1) + h] = jnp.concatenate(
                [flipped[low : low + rows // 2, :], flipped[low + rows // 2 : low + rows, :]], axis=1
            )
            n = 2 * (k - 1) + h
            fars.append(
                push(
                    turned.at[n],
                    from_far.at[2 * (k - 1) + core],
                    far_s.at[n],
                    far_r.at[2 * (k - 1) + core],
                    lax.rem(chip + k, chips) * 2 + h,
                )
            )
    gather_sums(1)
    gather_sums(2)
    for k in range(near):
        at = pl.multiple_of(lax.rem(chip + k, chips) * block, block)
        out_ref[:, pl.ds(at, block)] = held[0, :, k * block : (k + 1) * block]
    for copy in fars:
        copy.wait_send()
    for k in range(1, chips - near + 1):
        for c in range(2):
            n = 2 * (k - 1) + c
            pltpu.make_async_copy(from_far.at[n], from_far.at[n], far_r.at[n]).wait()
        at = pl.multiple_of(lax.rem(chip + chips - k, chips) * block, block)
        first, second = from_far[2 * k - 2], from_far[2 * k - 1]
        out_ref[: rows // 2, pl.ds(at, block)] = jnp.concatenate([first[:, :rows], second[:, :rows]], axis=1)
        out_ref[rows // 2 :, pl.ds(at, block)] = jnp.concatenate([first[:, rows:], second[:, rows:]], axis=1)
    for group in (cores, ys, zs):
        for copy in group.values():
            copy.wait_send()


def body(tiles, mu_list, lam_list, tile_count, coeff, owner):
    shards = lax.axis_size("aux")
    own_rows, occupied = coeff.shape
    nbasis = own_rows * shards
    _, slots, aux_local, block, _ = tiles.shape
    nblocks = nbasis // block
    depth_of_sum = aux_local * occupied
    scale = 1.0 / (depth_of_sum * shards)
    vmem = pl.BlockSpec(memory_space=pltpu.VMEM)
    dma = pltpu.SemaphoreType.DMA
    own = own_rows * 2 == block and nblocks % 4 == 0
    band = (nblocks // 2 + 1) * block if own else 0
    if own:
        whole_coeff = pl.pallas_call(
            functools.partial(gather_kernel, shards),
            out_shape=pltpu.VMEM((nbasis, occupied), coeff.dtype),
            in_specs=[vmem],
            out_specs=vmem,
            scratch_shapes=[dma((nblocks,))] * 4,
            compiler_params=pltpu.CompilerParams(collective_id=0, has_side_effects=True),
        )(coeff)
    else:
        whole_coeff = lax.all_gather(coeff, "aux", axis=0, tiled=True)
    wide = jnp.bfloat16 if own_rows % 16 == 0 else jnp.float32
    partial = pl.pallas_call(
        functools.partial(partial_kernel, shards, scale, own),
        out_shape=pltpu.VMEM((nbasis + band - block, depth_of_sum), jnp.bfloat16)
        if own
        else jax.ShapeDtypeStruct((nbasis, nbasis), jnp.float32),
        in_specs=[pl.BlockSpec(memory_space=pltpu.HBM)] * 5 + [vmem],
        out_specs=vmem,
        scratch_shapes=([] if own else [pltpu.VMEM((nbasis, depth_of_sum), wide)])
        + [
            pltpu.VMEM((aux_local * block, occupied), jnp.float32),
            pltpu.VMEM((slots, aux_local, block, block), tiles.dtype),
            pltpu.SMEM((slots,), jnp.int32),
            pltpu.SMEM((slots,), jnp.int32),
            pltpu.SMEM((1,), jnp.int32),
            pltpu.SMEM((shards,), jnp.int32),
            pltpu.SMEM((shards,), jnp.int32),
            dma((5,)),
        ],
        compiler_params=pltpu.CompilerParams(vmem_limit_bytes=(56 if own else 48) * 1024 * 1024),
    )(mu_list[0], lam_list[0], tile_count, owner, tiles[0], whole_coeff)
    if not own:
        return lax.psum_scatter(partial, "aux", scatter_dimension=0, tiled=True)
    depth = nblocks // 2
    far = nblocks - band // block
    f32 = jnp.float32
    return pl.pallas_call(
        functools.partial(scatter_kernel, shards, scale),
        out_shape=jax.ShapeDtypeStruct((own_rows, nbasis), f32),
        in_specs=[vmem],
        out_specs=vmem,
        scratch_shapes=[
            pltpu.VMEM((nblocks, block, band), f32),
            pltpu.VMEM((nblocks, own_rows, band), f32),
            pltpu.VMEM((depth, own_rows, band), f32),
            pltpu.VMEM((depth, own_rows, band), f32),
            pltpu.VMEM((depth, own_rows, band), f32),
            pltpu.VMEM((depth, own_rows, band), f32),
            pltpu.VMEM((2 * far, own_rows // 2, block), f32),
            pltpu.VMEM((2 * far, own_rows // 2, block), f32),
            dma((nblocks,)),
            dma((nblocks,)),
            dma((depth,)),
            dma((depth,)),
            dma((3 * depth,)),
            dma((3 * depth,)),
            dma((2 * far,)),
            dma((2 * far,)),
        ],
        compiler_params=pltpu.CompilerParams(
            collective_id=1, has_side_effects=True, vmem_limit_bytes=24 * 1024 * 1024
        ),
    )(partial)


def solution(mesh):
    return jax.shard_map(
        body,
        mesh=mesh,
        in_specs=(
            P(("parts", "aux"), None, None, None, None),
            P(("parts", "aux"), None),
            P(("parts", "aux"), None),
            P(("parts", "aux")),
            P(("parts", "aux"), None),
            P("parts"),
        ),
        out_specs=P(("parts", "aux"), None),
        check_vma=False,
    )
```

```python
import functools

import jax
import jax.numpy as jnp
from jax import lax
from jax.experimental import pallas as pl
from jax.experimental.pallas import tpu as pltpu
from jax.sharding import PartitionSpec as P

MESH = pl.DeviceIdType.MESH


def partial_kernel(
    shards, scale, own, mu_in, lam_in, count_in, owner_in, tiles_in, coeff_ref, out_ref, *rest
):
    *spare, total, tiles_ref, mu_ref, lam_ref, count_ref, owner_ref, place, sems = rest
    half = out_ref if own else spare[0]
    moves = [
        pltpu.make_async_copy(src, dst, sems.at[n])
        for n, (src, dst) in enumerate(
            (
                (mu_in, mu_ref),
                (lam_in, lam_ref),
                (count_in, count_ref),
                (owner_in, owner_ref),
                (tiles_in, tiles_ref),
            )
        )
    ]
    for move in moves:
        move.start()
    for move in moves[:4]:
        move.wait()
    slots, aux_local, block, _ = tiles_ref.shape
    nbasis, occupied = coeff_ref.shape
    nblocks = nbasis // block
    tile_rows = nbasis // shards
    count = count_ref[0]

    @pl.loop(0, shards)
    def _(d):
        place[owner_ref[d]] = d

    moves[4].wait()

    @pl.loop(0, nblocks)
    def _(b):
        def add(t, seen):
            hit = (mu_ref[t] == b) & (t < count)

            def term():
                start = pl.multiple_of(lam_ref[t] * block, block)
                return jnp.dot(
                    tiles_ref[t].reshape(aux_local * block, block),
                    coeff_ref[pl.ds(start, block), :],
                    preferred_element_type=jnp.float32,
                )

            @pl.when(hit & (seen == 0))
            def _():
                total[...] = term()

            @pl.when(hit & (seen > 0))
            def _():
                total[...] += term()

            return seen + hit.astype(jnp.int32)

        seen = lax.fori_loop(0, slots, add, jnp.int32(0))
        pieces = max(block // tile_rows, 1)
        rows = block // pieces
        per_tile = tile_rows // rows
        for piece in range(pieces):
            at = b * pieces + piece
            where = pl.multiple_of(place[at // per_tile] * tile_rows + lax.rem(at, per_tile) * rows, rows)

            @pl.when(seen > 0)
            def _():
                for p in range(aux_local):
                    value = total[p * block + piece * rows : p * block + (piece + 1) * rows, :]
                    half[pl.ds(where, rows), p * occupied : (p + 1) * occupied] = value.astype(
                        jnp.bfloat16
                    ).astype(half.dtype)

            @pl.when(seen == 0)
            def _():
                half[pl.ds(where, rows), :] = jnp.zeros((rows, aux_local * occupied), half.dtype)

            if own:

                @pl.when(where < half.shape[0] - nbasis)
                def _():
                    again = pl.multiple_of(where + nbasis, rows)
                    half[pl.ds(again, rows), :] = half[pl.ds(where, rows), :]

    if not own:

        @pl.loop(0, nblocks)
        def _(d):
            start = pl.multiple_of(d * block, block)
            out_ref[pl.ds(start, block), :] = (
                lax.dot_general(
                    half[pl.ds(start, block), :].astype(jnp.bfloat16),
                    half[...].astype(jnp.bfloat16),
                    (((1,), (1,)), ((), ())),
                    preferred_element_type=jnp.float32,
                )
                * scale
            )


def greet(me, shards):
    barrier = pltpu.get_barrier_semaphore()
    for k in range(1, shards):
        pl.semaphore_signal(barrier, inc=1, device_id={"aux": lax.rem(me + k, shards)}, device_id_type=MESH)
    return lambda: pl.semaphore_wait(barrier, shards - 1)


def push(src, dst, send, recv, device):
    copy = pltpu.make_async_remote_copy(
        src_ref=src, dst_ref=dst, send_sem=send, recv_sem=recv, device_id={"aux": device}, device_id_type=MESH
    )
    copy.start()
    return copy


def gather_kernel(shards, coeff_ref, out_ref, send, recv, pass_send, pass_recv):
    me = lax.axis_index("aux")
    rows = coeff_ref.shape[0]
    chips = shards // 2
    chip, core = me // 2, lax.rem(me, 2)
    sibling = chip * 2 + 1 - core

    def rows_of(device):
        return out_ref.at[pl.ds(pl.multiple_of(device * rows, rows), rows), :]

    met = greet(me, shards)
    out_ref[pl.ds(pl.multiple_of(me * rows, rows), rows), :] = coeff_ref[...]
    met()
    copies = {}
    near_first = sorted(range(1, chips), key=lambda k: min(k, chips - k))
    for k in near_first[::-1]:
        target = lax.rem(chip + k, chips) * 2 + core
        copies[k] = push(coeff_ref, rows_of(me), send.at[k], recv.at[k], target)
    passed = [push(coeff_ref, rows_of(me), pass_send.at[0], pass_recv.at[0], sibling)]
    for k in near_first:
        copies[k].wait_recv()
        source = lax.rem(chip + chips - k, chips) * 2 + core
        passed.append(push(rows_of(source), rows_of(source), pass_send.at[k], pass_recv.at[k], sibling))
    for copy in copies.values():
        copy.wait_send()
    for copy in passed:
        copy.wait()


def scatter_kernel(
    shards, scale, half_ref, out_ref, part_ref, from_core, to_y, from_y, held, from_z, turned, from_far, core_s, core_r, y_s, y_r, z_s, z_r, far_s, far_r
):
    me = lax.axis_index("aux")
    chips, block, band = part_ref.shape
    rows = block // 2
    depth = chips // 2
    chip, core = me // 2, lax.rem(me, 2)
    z, y = chip // 2, lax.rem(chip, 2)
    sibling = chip * 2 + 1 - core
    mine = pl.ds(pl.multiple_of(core * rows, rows), rows)
    theirs = pl.ds(pl.multiple_of((1 - core) * rows, rows), rows)
    offsets = list(range(depth // 2, 0, -1)) + list(range(depth // 2 + 1, depth)) + [0]

    met = greet(me, shards)
    cores, ys = {}, {}

    def multiply(k, v):
        n = 2 * k + v
        d = lax.rem(z + k, depth) * 2 + (y if v == 0 else 1 - y)
        start = pl.multiple_of(d * block, block)
        part_ref[n] = (
            lax.dot_general(
                half_ref[pl.ds(start, block), :],
                half_ref[pl.ds(start, band), :],
                (((1,), (1,)), ((), ())),
                preferred_element_type=jnp.float32,
            )
            * scale
        )
        if (k, v) == (offsets[0], 1):
            met()
        cores[k, v] = push(part_ref.at[n, theirs, :], from_core.at[n], core_s.at[n], core_r.at[n], sibling)

    def send_on(k):
        cores[k, 1].wait_recv()
        to_y[k] = part_ref[2 * k + 1, mine, :] + from_core[2 * k + 1]
        ys[k] = push(to_y.at[k], from_y.at[k], y_s.at[k], y_r.at[k], (z * 2 + 1 - y) * 2 + core)

    before = None
    for k in offsets:
        multiply(k, 1)
        if before is not None:
            send_on(before)
        before = k
    send_on(before)
    for k in offsets:
        multiply(k, 0)
    zs = {}
    near = band // block
    middle = (chips - near + 1) * block
    pieces = ((block, middle), (0, block), (middle, band))
    for k in offsets:
        cores[k, 0].wait_recv()
        ys[k].wait_recv()
        held[k] = part_ref[2 * k, mine, :] + from_core[2 * k] + from_y[k]
        if k:
            for i, (low, high) in enumerate(pieces):
                zs[k, i] = push(
                    held.at[k, :, low:high],
                    from_z.at[k, :, low:high],
                    z_s.at[3 * k + i],
                    z_r.at[3 * k + i],
                    (lax.rem(z + k, depth) * 2 + y) * 2 + core,
                )

    def gather_sums(i):
        low, high = pieces[i]
        for k in offsets[:-1]:
            zs[k, i].wait_recv()
            held[0, :, low:high] += from_z[k, :, low:high]

    gather_sums(0)
    fars = []
    for k in range(1, chips - near + 1):
        flipped = held[0, :, k * block : (k + 1) * block].T
        for h in range(2):
            low = h * rows
            turned[2 * (k - 1) + h] = jnp.concatenate(
                [flipped[low : low + rows // 2, :], flipped[low + rows // 2 : low + rows, :]], axis=1
            )
            n = 2 * (k - 1) + h
            fars.append(
                push(
                    turned.at[n],
                    from_far.at[2 * (k - 1) + core],
                    far_s.at[n],
                    far_r.at[2 * (k - 1) + core],
                    lax.rem(chip + k, chips) * 2 + h,
                )
            )
    gather_sums(1)
    gather_sums(2)
    for k in range(near):
        at = pl.multiple_of(lax.rem(chip + k, chips) * block, block)
        out_ref[:, pl.ds(at, block)] = held[0, :, k * block : (k + 1) * block]
    for copy in fars:
        copy.wait_send()
    for k in range(1, chips - near + 1):
        for c in range(2):
            n = 2 * (k - 1) + c
            pltpu.make_async_copy(from_far.at[n], from_far.at[n], far_r.at[n]).wait()
        at = pl.multiple_of(lax.rem(chip + chips - k, chips) * block, block)
        first, second = from_far[2 * k - 2], from_far[2 * k - 1]
        out_ref[: rows // 2, pl.ds(at, block)] = jnp.concatenate([first[:, :rows], second[:, :rows]], axis=1)
        out_ref[rows // 2 :, pl.ds(at, block)] = jnp.concatenate([first[:, rows:], second[:, rows:]], axis=1)
    for group in (cores, ys, zs):
        for copy in group.values():
            copy.wait_send()


def body(tiles, mu_list, lam_list, tile_count, coeff, owner):
    shards = lax.axis_size("aux")
    own_rows, occupied = coeff.shape
    nbasis = own_rows * shards
    _, slots, aux_local, block, _ = tiles.shape
    nblocks = nbasis // block
    depth_of_sum = aux_local * occupied
    scale = 1.0 / (depth_of_sum * shards)
    vmem = pl.BlockSpec(memory_space=pltpu.VMEM)
    dma = pltpu.SemaphoreType.DMA
    own = own_rows * 2 == block and nblocks % 4 == 0
    band = (nblocks // 2 + 1) * block if own else 0
    if own:
        whole_coeff = pl.pallas_call(
            functools.partial(gather_kernel, shards),
            out_shape=pltpu.VMEM((nbasis, occupied), coeff.dtype),
            in_specs=[vmem],
            out_specs=vmem,
            scratch_shapes=[dma((nblocks,))] * 4,
            compiler_params=pltpu.CompilerParams(collective_id=0, has_side_effects=True),
        )(coeff)
    else:
        whole_coeff = lax.all_gather(coeff, "aux", axis=0, tiled=True)
    wide = jnp.bfloat16 if own_rows % 16 == 0 else jnp.float32
    partial = pl.pallas_call(
        functools.partial(partial_kernel, shards, scale, own),
        out_shape=pltpu.VMEM((nbasis + band - block, depth_of_sum), jnp.bfloat16)
        if own
        else jax.ShapeDtypeStruct((nbasis, nbasis), jnp.float32),
        in_specs=[pl.BlockSpec(memory_space=pltpu.HBM)] * 5 + [vmem],
        out_specs=vmem,
        scratch_shapes=([] if own else [pltpu.VMEM((nbasis, depth_of_sum), wide)])
        + [
            pltpu.VMEM((aux_local * block, occupied), jnp.float32),
            pltpu.VMEM((slots, aux_local, block, block), tiles.dtype),
            pltpu.SMEM((slots,), jnp.int32),
            pltpu.SMEM((slots,), jnp.int32),
            pltpu.SMEM((1,), jnp.int32),
            pltpu.SMEM((shards,), jnp.int32),
            pltpu.SMEM((shards,), jnp.int32),
            dma((5,)),
        ],
        compiler_params=pltpu.CompilerParams(vmem_limit_bytes=(56 if own else 48) * 1024 * 1024),
    )(mu_list[0], lam_list[0], tile_count, owner, tiles[0], whole_coeff)
    if not own:
        return lax.psum_scatter(partial, "aux", scatter_dimension=0, tiled=True)
    depth = nblocks // 2
    far = nblocks - band // block
    f32 = jnp.float32
    return pl.pallas_call(
        functools.partial(scatter_kernel, shards, scale),
        out_shape=jax.ShapeDtypeStruct((own_rows, nbasis), f32),
        in_specs=[vmem],
        out_specs=vmem,
        scratch_shapes=[
            pltpu.VMEM((nblocks, block, band), f32),
            pltpu.VMEM((nblocks, own_rows, band), f32),
            pltpu.VMEM((depth, own_rows, band), f32),
            pltpu.VMEM((depth, own_rows, band), f32),
            pltpu.VMEM((depth, own_rows, band), f32),
            pltpu.VMEM((depth, own_rows, band), f32),
            pltpu.VMEM((2 * far, own_rows // 2, block), f32),
            pltpu.VMEM((2 * far, own_rows // 2, block), f32),
            dma((nblocks,)),
            dma((nblocks,)),
            dma((depth,)),
            dma((depth,)),
            dma((3 * depth,)),
            dma((3 * depth,)),
            dma((2 * far,)),
            dma((2 * far,)),
        ],
        compiler_params=pltpu.CompilerParams(
            collective_id=1, has_side_effects=True, vmem_limit_bytes=24 * 1024 * 1024
        ),
    )(partial)


def solution(mesh):
    return jax.shard_map(
        body,
        mesh=mesh,
        in_specs=(
            P(("parts", "aux"), None, None, None, None),
            P(("parts", "aux"), None),
            P(("parts", "aux"), None),
            P(("parts", "aux")),
            P(("parts", "aux"), None),
            P("parts"),
        ),
        out_specs=P(("parts", "aux"), None),
        check_vma=False,
    )
```
